32 devices in a mesh: scen: 4 (over x, core), own: 8 (over z, y).
Axes of the slice: x: 2, y: 2, z: 4, core: 2. Of those that a mesh axis runs over, the one named last changes fastest.
Arguments:
- kinv: bfloat16 [128, 1024, 1024], P(('scen', 'own'))
- coupling: bfloat16 [128, 1024, 768], P(('scen', 'own')), may hold values from -0.09375 to 0.09375
- residual: float32 [128, 1024], P(('scen', 'own')), may hold values from -6 to 6
- first_step: float32 [16384], P('own'), may hold values from -6 to 6
- links: int32 [128, 6], P(('scen', 'own')), may hold values from 0 to 127, as said below
- counts: int32 [128], P(('scen', 'own')), may hold values from 2 to 6
- owner_map: int32 [128], replicated, may hold values from 0 to 7, as said below
Outputs:
- schur_band: float32 [8, 2048, 1920], P('own', 'scen')
- second_step: float32 [128, 1024], P(('scen', 'own'))
The draws below stay inside these ranges and needn't reach their ends.
Inputs may be any that keep to these rules, and one draw needn't show every extreme that they name: `owner_map`: every 8 consecutive linking blocks have distinct owners, and each owner has 16 blocks. `links`: the 6 slots of a scenario name distinct blocks. The 4 scenarios of one device couple only to blocks of one run of 8 consecutive linking blocks, and all of them name one common block in slot 0.
All inputs are finite; a program needn't handle non-finite values.
Results may differ from the reference program's by a relative error of at most 0.003.
Values may be sent and summed in bfloat16 or wider, within the bound.
A program may use at most 192 MiB of HBM per device.

```python
import math
import jax
import jax.numpy as jnp
from jax import lax

BS = 128
NB = 128
K = 6
W = 8
R = 1024
SC_DEV = 4
SCEN = 128
OWNERS = 8
N_OWN = 8


def draw_owner_map(key, part):
    shuffled = jax.random.permutation(jax.random.fold_in(key, 11), OWNERS).astype(jnp.int32)
    return shuffled[jnp.arange(NB, dtype=jnp.int32) % OWNERS]


def draw_links(key, part):
    device_total = SCEN // SC_DEV
    key_start, key_anchor, key_shuffle, key_edges = jax.random.split(jax.random.fold_in(key, 21), 4)
    window_starts = jax.random.randint(key_start, (device_total,), 0, NB - W + 1)
    anchors = jax.random.randint(key_anchor, (device_total,), 0, W)
    edge_devices = jax.random.permutation(key_edges, device_total)[:2]
    window_starts = window_starts.at[edge_devices[0]].set(0).at[edge_devices[1]].set(NB - W)
    anchors = anchors.at[edge_devices[0]].set(0).at[edge_devices[1]].set(W - 1)
    scen_keys = jax.random.split(key_shuffle, SCEN)
    shuffled = jax.vmap(lambda scen_key: jax.random.permutation(scen_key, W))(scen_keys)
    device_of = jnp.arange(SCEN, dtype=jnp.int32) // SC_DEV
    anchor_of = anchors[device_of]
    sort_keys = jnp.where(shuffled == anchor_of[:, None], -1, jnp.arange(W, dtype=jnp.int32)[None, :])
    ordering = jnp.argsort(sort_keys, axis=1, stable=True)
    chosen = jnp.take_along_axis(shuffled, ordering, axis=1)[:, :K]
    return (window_starts[device_of][:, None] + chosen).astype(jnp.int32)


def draw_counts(key, part):
    key_counts, key_full = jax.random.split(jax.random.fold_in(key, 31))
    drawn = jax.random.randint(key_counts, (SCEN,), 2, K + 1)
    full_index = jax.random.randint(key_full, (), 0, SCEN)
    return jnp.where(jnp.arange(SCEN) == full_index, K, drawn).astype(jnp.int32)


def draw_kinv(key, part):
    base_key = jax.random.fold_in(key, 41)

    def per_scenario(scen_index):
        scen_key = jax.random.fold_in(base_key, scen_index)
        key_noise, key_diag = jax.random.split(scen_key)
        noise_draw = jax.random.normal(key_noise, (R, R), jnp.float32)
        diag_draw = jax.random.uniform(key_diag, (R,), jnp.float32, 0.5, 1.5)
        matrix = noise_draw * (0.6 / math.sqrt(R))
        return (matrix + jnp.diag(diag_draw)).astype(jnp.bfloat16)
    return lax.map(per_scenario, jnp.arange(SCEN, dtype=jnp.int32))


def block_scale(stream_key, shape, shards, low, largest):
    level = 1.0
    for dim, parts in shards:
        steps = jax.random.uniform(jax.random.fold_in(jax.random.fold_in(stream_key, 6), dim), (parts,), jnp.float32, low / len(shards), largest / len(shards))
        level = level * jnp.repeat(jnp.exp(steps), shape[dim] // parts).reshape((-1,) + (1,) * (len(shape) - 1 - dim))
    return level


def centred(stream_key, shape, width, most, cuts=(), held_as=jnp.bfloat16):
    values = width * jax.random.normal(stream_key, shape, jnp.float32)
    if cuts:
        values = values * block_scale(stream_key, shape, cuts, -0.22, 0.18)
    return jnp.clip(values, -most, most).astype(held_as)


def setup_inputs(seed: int = 0) -> dict:
    seeds = jax.random.split(jax.random.key(seed), 8)
    kinv = draw_kinv(jax.random.fold_in(seeds[7], 71), 0)
    coupling = centred(seeds[1], (SCEN, R, K * BS), (4 * R) ** -0.5, 0.09375, ((0, 32),))
    residual = centred(seeds[2], (SCEN, R), 1.0, 6.0, ((0, 32),), jnp.float32)
    first_step = centred(seeds[3], (NB * BS,), 1.0, 6.0, ((0, 8),), jnp.float32)
    links = draw_links(jax.random.fold_in(seeds[7], 71), 0)
    counts = draw_counts(jax.random.fold_in(seeds[7], 71), 0)
    owner_map = draw_owner_map(jax.random.fold_in(seeds[7], 71), 0)
    return dict(kinv=kinv, coupling=coupling, residual=residual, first_step=first_step, links=links, counts=counts, owner_map=owner_map)


def reference(kinv, coupling, residual, first_step, links, counts, owner_map):
    band_width = 2 * W - 1
    step_table = first_step.reshape(NB, BS)

    def per_scenario(band_total, inputs):
        kinv_one, coupling_one, residual_one, links_one, count_one = inputs
        live_slots = jnp.arange(K, dtype=jnp.int32) < count_one
        coupled = jnp.where(live_slots[None, :, None], coupling_one.reshape(R, K, BS), 0).reshape(R, K * BS).astype(jnp.bfloat16)
        solved = jnp.dot(kinv_one, coupled, preferred_element_type=jnp.float32).astype(jnp.bfloat16)
        contrib = jnp.dot(coupled.T, solved, preferred_element_type=jnp.float32)
        blocks = contrib.reshape(K, BS, K, BS).transpose(0, 2, 1, 3)
        row_ids = jnp.broadcast_to(links_one[:, None], (K, K)).astype(jnp.int32)
        offset_ids = (links_one[None, :] - links_one[:, None] + (W - 1)).astype(jnp.int32)
        band_total = band_total.at[row_ids, offset_ids].add(blocks)
        picked = step_table[links_one].reshape(K * BS).astype(jnp.bfloat16)
        product = jnp.dot(coupled, picked, preferred_element_type=jnp.float32)
        reduced_rhs = (residual_one - product).astype(jnp.bfloat16)
        second = jnp.dot(kinv_one, reduced_rhs, preferred_element_type=jnp.float32)
        return band_total, second

    start_band = jnp.zeros((NB, band_width, BS, BS), jnp.float32)
    band_total, second_step = lax.scan(per_scenario, start_band, (kinv, coupling, residual, links, counts))
    positions = jnp.arange(NB, dtype=jnp.int32)
    same_owner = owner_map[:, None] == owner_map[None, :]
    earlier = positions[None, :] < positions[:, None]
    owner_rank = jnp.sum(same_owner & earlier, axis=1).astype(jnp.int32)
    row_blocks = NB // N_OWN
    arranged = jnp.zeros((N_OWN, row_blocks, band_width, BS, BS), jnp.float32).at[owner_map, owner_rank].set(band_total)
    schur_band = arranged.transpose(0, 1, 3, 2, 4).reshape(N_OWN, row_blocks * BS, band_width * BS)
    return schur_band, second_step
```

```python
import functools

import jax
import jax.numpy as jnp
from jax import lax
from jax.experimental import pallas as pl
from jax.experimental.pallas import tpu as pltpu
from jax.sharding import PartitionSpec as P

BS = 128
NB = 128
K = 6
W = 8
R = 1024
BAND = (2 * W - 1) * BS
WIN = W * BS
MESH = pl.DeviceIdType.MESH
TN = (((0,), (0,)), ((), ()))
NT = (((1,), (1,)), ((), ()))


def window_kernel(rows_ref, cols_ref, counts_ref, kinv_ref, coup_ref, out_ref, win):
    s = pl.program_id(0)

    @pl.when(s == 0)
    def _():
        win[...] = jnp.zeros_like(win)

    count = counts_ref[s]
    slot = lax.broadcasted_iota(jnp.int32, (R, K * BS), 1) // BS
    coupled = jnp.where(slot < count, coup_ref[0], jnp.zeros((), jnp.bfloat16))
    solved = jnp.dot(kinv_ref[0], coupled, preferred_element_type=jnp.float32)
    solved = solved.astype(jnp.bfloat16)
    for i in range(K):

        @pl.when(i < count)
        def _():
            strip = lax.dot_general(
                coup_ref[0, :, i * BS : (i + 1) * BS],
                solved,
                TN,
                preferred_element_type=jnp.float32,
            )
            row = pl.multiple_of(rows_ref[s * K + i] * BS, BS)
            for j in range(K):
                col = pl.multiple_of(cols_ref[s * K + j] * BS, BS)
                win[pl.ds(row, BS), pl.ds(col, BS)] += strip[:, j * BS : (j + 1) * BS]

    @pl.when(s == pl.num_programs(0) - 1)
    def _():
        out_ref[...] = win[...].astype(jnp.bfloat16)


def windows(rows, cols, counts, kinv, coupling, owners):
    scen_count = kinv.shape[0]
    return pl.pallas_call(
        window_kernel,
        out_shape=jax.ShapeDtypeStruct((owners * BS, WIN), jnp.bfloat16),
        grid_spec=pltpu.PrefetchScalarGridSpec(
            num_scalar_prefetch=3,
            grid=(scen_count,),
            in_specs=[
                pl.BlockSpec((1, R, R), lambda s, *_: (s, 0, 0)),
                pl.BlockSpec((1, R, K * BS), lambda s, *_: (s, 0, 0)),
            ],
            out_specs=pl.BlockSpec((owners * BS, WIN), lambda s, *_: (0, 0)),
            scratch_shapes=[pltpu.VMEM((owners * BS, WIN), jnp.float32)],
        ),
        compiler_params=pltpu.CompilerParams(vmem_limit_bytes=56 * 2**20),
    )(rows, cols, counts, kinv, coupling)


def flip(index, bits, size):
    result = 0
    weight = 1
    while weight < size:
        bit = (index // weight) % 2
        if (bits // weight) % 2:
            bit = 1 - bit
        result = result + bit * weight
        weight *= 2
    return result


def exchange_kernel(
    groups, owners, rows_ref, meta_ref, all_rows, all_meta,
    own_send, own_recv, x_send, x_recv, core_send, core_recv,
    meta_send, meta_recv, meta2_send, meta2_recv, local_sem,
):
    g = lax.axis_index("scen")
    o = lax.axis_index("own")
    chips = groups // 2
    core = g % 2
    x = g // 2
    sibling = x * 2 + 1 - core
    xs = [flip(x, b, chips) * 2 + core for b in range(chips)]
    partner = [flip(o, k, owners) for k in range(owners)]

    barrier = pltpu.get_barrier_semaphore()
    for k in range(1, owners):
        pl.semaphore_signal(barrier, inc=1, device_id=(g, partner[k]), device_id_type=MESH)
    others = [flip(g, b, groups) for b in range(1, groups)]
    for other in others:
        pl.semaphore_signal(barrier, inc=1, device_id=(other, o), device_id_type=MESH)
    pl.semaphore_wait(barrier, owners - 1 + groups - 1)

    def remote(src, dst, send, recv, device):
        return pltpu.make_async_remote_copy(
            src_ref=src, dst_ref=dst, send_sem=send, recv_sem=recv,
            device_id=device, device_id_type=MESH,
        )

    own = [None] * owners
    for k in range(1, owners):
        own[k] = remote(
            rows_ref.at[partner[k]], all_rows.at[g, o], own_send.at[k], own_recv.at[k], (g, partner[k])
        )
    meta = [None] * owners
    for k in range(1, owners):
        meta[k] = remote(
            meta_ref, all_meta.at[g, o], meta_send.at[k], meta_recv.at[k], (g, partner[k])
        )
    keep_rows = pltpu.make_async_copy(rows_ref.at[o], all_rows.at[g, o], local_sem.at[0])
    keep_meta = pltpu.make_async_copy(meta_ref, all_meta.at[g, o], local_sem.at[1])

    far = list(range(owners // 2, owners))
    near = list(range(1, owners // 2))
    keep_meta.start()
    for k in range(1, owners):
        meta[k].start()
    own[far[0]].start()
    own[far[1]].start()
    keep_rows.start()
    for k in near:
        own[k].start()

    x_copies = {}
    core_copies = {}

    def forward(k):
        h = partner[k]
        src = rows_ref.at[o] if k == 0 else all_rows.at[g, h]
        for b in range(1, chips):
            x_copies[b, k] = remote(
                src, all_rows.at[g, h], x_send.at[b, k], x_recv.at[b, k], (xs[b], o)
            )
            x_copies[b, k].start()
        core_copies[0, k] = remote(
            src, all_rows.at[g, h], core_send.at[0, k], core_recv.at[0, k], (sibling, o)
        )
        core_copies[0, k].start()

    def forward_x(k):
        h = partner[k]
        for b in range(1, chips):
            x_copies[b, k].wait_recv()
            place = all_rows.at[xs[b], h]
            core_copies[b, k] = remote(
                place, place, core_send.at[b, k], core_recv.at[b, k], (sibling, o)
            )
            core_copies[b, k].start()

    forward(0)
    meta2 = []
    keep_meta.wait()
    for k in range(1, owners):
        meta[k].wait()
    for b, other in enumerate(others):
        copy = remote(
            all_meta.at[g], all_meta.at[g], meta2_send.at[b], meta2_recv.at[b], (other, o)
        )
        copy.start()
        meta2.append(copy)
    done = [0]
    for k in near:
        own[k].wait_recv()
        forward(k)
        done.append(k)
    behind = 0
    for n, k in enumerate(far):
        if n + 2 < len(far):
            own[k].wait_send()
            own[far[n + 2]].start()
        own[k].wait_recv()
        forward(k)
        done.append(k)
        while behind < len(done) - 2:
            forward_x(done[behind])
            behind += 1
    while behind < len(done):
        forward_x(done[behind])
        behind += 1
    for copy in meta2:
        copy.wait()
    keep_rows.wait()
    for k in near + far[-2:]:
        own[k].wait_send()
    for k in range(owners):
        for b in range(1, chips):
            x_copies[b, k].wait_send()
        for b in range(chips):
            core_copies[b, k].wait()


def exchange(rows, meta, groups, owners):
    any_space = pl.BlockSpec(memory_space=pl.ANY)
    dma = pltpu.SemaphoreType.DMA
    return pl.pallas_call(
        functools.partial(exchange_kernel, groups, owners),
        out_shape=(
            jax.ShapeDtypeStruct((groups, owners, BS, WIN), jnp.bfloat16),
            jax.ShapeDtypeStruct((groups, owners) + meta.shape, jnp.float32),
        ),
        in_specs=[any_space, any_space],
        out_specs=(any_space, any_space),
        scratch_shapes=[
            dma((owners,)), dma((owners,)),
            dma((groups // 2, owners)), dma((groups // 2, owners)),
            dma((groups // 2, owners)), dma((groups // 2, owners)),
            dma((owners,)), dma((owners,)),
            dma((groups,)), dma((groups,)),
            dma((2,)),
        ],
        compiler_params=pltpu.CompilerParams(collective_id=0, has_side_effects=True),
    )(rows, meta)


def place_kernel(
    blocks, sources, codes_ref, links_ref, counts_ref, base_ref,
    kinv_ref, coup_ref, residual_ref, table_ref, rows_ref, band_ref, step_ref, held, sems,
):
    s = pl.program_id(0)
    base = base_ref[0]

    def copy_of(n):
        return pltpu.make_async_copy(rows_ref.at[n], held.at[n], sems.at[n])

    @pl.when(s == 0)
    def _():
        def begin(n, carry):
            rank = codes_ref[n] // W - base

            @pl.when((codes_ref[n] >= 0) & (rank >= 0) & (rank < blocks))
            def _():
                copy_of(n).start()

            return carry

        lax.fori_loop(0, sources, begin, 0)

    count = counts_ref[s]
    parts = []
    for k in range(K):
        row = table_ref[pl.ds(links_ref[s * K + k], 1), :]
        parts.append(jnp.where(k < count, row, 0.0))
    picked = jnp.broadcast_to(jnp.concatenate(parts, axis=1), (16, K * BS)).astype(jnp.bfloat16)
    product = lax.dot_general(picked, coup_ref[0], NT, preferred_element_type=jnp.float32)
    reduced = (residual_ref[pl.ds(s, 1), :] - product).astype(jnp.bfloat16)
    step = lax.dot_general(reduced, kinv_ref[0], NT, preferred_element_type=jnp.float32)
    step_ref[pl.ds(s, 1), :] = step[:1]

    @pl.when(s < blocks)
    def _():
        band_ref[...] = jnp.zeros_like(band_ref)

        def add(n, carry):
            code = codes_ref[n]

            @pl.when((code >= 0) & (code // W - base == s))
            def _():
                copy_of(n).wait()
                col = pl.multiple_of((W - 1 - code % W) * BS, BS)
                band_ref[:, pl.ds(col, WIN)] += held[n].astype(jnp.float32)

            return carry

        lax.fori_loop(0, sources, add, 0)


def place(codes, links, counts, base, kinv, coupling, residual, table, rows, blocks):
    scen_count = kinv.shape[0]
    sources = rows.shape[0]
    assert blocks <= scen_count
    return pl.pallas_call(
        functools.partial(place_kernel, blocks, sources),
        out_shape=(
            jax.ShapeDtypeStruct((blocks * BS, BAND), jnp.float32),
            jax.ShapeDtypeStruct((scen_count, R), jnp.float32),
        ),
        grid_spec=pltpu.PrefetchScalarGridSpec(
            num_scalar_prefetch=4,
            grid=(scen_count,),
            in_specs=[
                pl.BlockSpec((1, R, R), lambda s, *_: (s, 0, 0)),
                pl.BlockSpec((1, R, K * BS), lambda s, *_: (s, 0, 0)),
                pl.BlockSpec((scen_count, R), lambda s, *_: (0, 0)),
                pl.BlockSpec((NB, BS), lambda s, *_: (0, 0)),
                pl.BlockSpec(memory_space=pl.ANY),
            ],
            out_specs=(
                pl.BlockSpec((BS, BAND), lambda s, *_: (jnp.minimum(s, blocks - 1), 0)),
                pl.BlockSpec((scen_count, R), lambda s, *_: (0, 0)),
            ),
            scratch_shapes=[
                pltpu.VMEM((sources, BS, WIN), jnp.bfloat16),
                pltpu.SemaphoreType.DMA((sources,)),
            ],
        ),
        compiler_params=pltpu.CompilerParams(vmem_limit_bytes=58 * 2**20),
    )(codes, links, counts, base, kinv, coupling, residual, table, rows)


def local(kinv, coupling, residual, first_step, links, counts, owner_map):
    groups = lax.axis_size("scen")
    owners = lax.axis_size("own")
    row_blocks = NB // owners
    blocks = row_blocks // groups
    positions = jnp.arange(NB, dtype=jnp.int32)
    same_owner = owner_map[:, None] == owner_map[None, :]
    rank = jnp.sum(same_owner & (positions[None, :] < positions[:, None]), axis=1, dtype=jnp.int32)
    start = jnp.min(links)
    inside = (positions >= start) & (positions < start + W)
    lanes = jnp.arange(BS, dtype=jnp.int32)
    holds = inside[:, None] & (owner_map[:, None] == lanes[None, :])
    codes = jnp.sum(jnp.where(holds, (rank * W + positions - start + 1)[:, None], 0), axis=0) - 1
    flat_links = links.reshape(-1)
    owner_of = jnp.sum(
        jnp.where(flat_links[:, None] == positions[None, :], owner_map[None, :], 0), axis=1
    )
    rows = windows(owner_of, flat_links - start, counts, kinv, coupling, owners)
    table_rows = first_step.shape[0] // BS
    meta = jnp.concatenate(
        [
            first_step.reshape(table_rows, BS),
            jnp.broadcast_to(codes.astype(jnp.float32)[None], (8, BS)),
        ],
        axis=0,
    )
    all_rows, all_meta = exchange(rows.reshape(owners, BS, WIN), meta, groups, owners)
    g = lax.axis_index("scen")
    o = lax.axis_index("own")
    table = all_meta[0, :, :table_rows].reshape(NB, BS)
    mine = jnp.sum(
        jnp.where(lanes == o, all_meta[:, :, table_rows].reshape(groups * owners, BS), 0.0), axis=1
    ).astype(jnp.int32)
    band, second_step = place(
        mine, flat_links, counts, (g * blocks).reshape(1), kinv, coupling, residual, table,
        all_rows.reshape(groups * owners, BS, WIN), blocks,
    )
    return band[None], second_step


def solution(mesh):
    placed = (
        P(("scen", "own"), None, None),
        P(("scen", "own"), None, None),
        P(("scen", "own"), None),
        P("own"),
        P(("scen", "own"), None),
        P(("scen", "own")),
        P(),
    )
    return jax.shard_map(
        local,
        mesh=mesh,
        in_specs=placed,
        out_specs=(P("own", "scen", None), P(("scen", "own"), None)),
        check_vma=False,
    )
```

```python
import functools

import jax
import jax.numpy as jnp
from jax import lax
from jax.experimental import pallas as pl
from jax.experimental.pallas import tpu as pltpu
from jax.sharding import PartitionSpec as P

BS = 128
NB = 128
K = 6
W = 8
R = 1024
BAND = (2 * W - 1) * BS
WIN = W * BS
MESH = pl.DeviceIdType.MESH
TN = (((0,), (0,)), ((), ()))
NT = (((1,), (1,)), ((), ()))


def window_kernel(
    links_ref, counts_ref, map_ref, map_row_ref, kinv_ref, coup_ref, out_ref, codes_ref, win
):
    s = pl.program_id(0)
    scens = pl.num_programs(0)
    start = lax.fori_loop(
        0, scens * K, lambda n, low: jnp.minimum(low, links_ref[n // K, n % K]), NB - 1
    )

    @pl.when(s == 0)
    def _():
        win[...] = jnp.zeros_like(win)
        lane = lax.broadcasted_iota(jnp.int32, (1, BS), 1)
        map_row = map_row_ref[...]
        codes = jnp.full((1, BS), -1, jnp.int32)
        for w in range(W):
            block = start + w
            owner = map_ref[jnp.minimum(block, NB - 1)]
            earlier = (map_row == owner) & (lane < block)
            rank = jnp.sum(jnp.where(earlier, 1.0, 0.0), axis=1, keepdims=True).astype(jnp.int32)
            codes = jnp.where((lane == owner) & (block < NB), rank * W + w, codes)
        codes_ref[...] = codes

    count = counts_ref[s]
    slot = lax.broadcasted_iota(jnp.int32, (R, K * BS), 1) // BS
    coupled = jnp.where(slot < count, coup_ref[0], jnp.zeros((), jnp.bfloat16))
    solved = jnp.dot(kinv_ref[0], coupled, preferred_element_type=jnp.float32)
    solved = solved.astype(jnp.bfloat16)
    for i in range(0, K, 2):

        @pl.when(i < count)
        def _():
            strip = lax.dot_general(
                coupled[:, i * BS : (i + 2) * BS], solved, TN, preferred_element_type=jnp.float32
            )
            for n in range(2):
                row = pl.multiple_of(map_ref[links_ref[s, i + n]] * BS, BS)
                for j in range(K):
                    col = pl.multiple_of((links_ref[s, j] - start) * BS, BS)
                    win[pl.ds(row, BS), pl.ds(col, BS)] += strip[
                        n * BS : (n + 1) * BS, j * BS : (j + 1) * BS
                    ]

    @pl.when(s == scens - 1)
    def _():
        out_ref[...] = win[...].astype(jnp.bfloat16)


def windows(links, counts, owner_map, kinv, coupling, owners):
    scen_count = kinv.shape[0]
    return pl.pallas_call(
        window_kernel,
        out_shape=(
            jax.ShapeDtypeStruct((owners * BS, WIN), jnp.bfloat16),
            jax.ShapeDtypeStruct((1, BS), jnp.int32),
        ),
        grid_spec=pltpu.PrefetchScalarGridSpec(
            num_scalar_prefetch=3,
            grid=(scen_count,),
            in_specs=[
                pl.BlockSpec((1, NB), lambda s, *_: (0, 0)),
                pl.BlockSpec((1, R, R), lambda s, *_: (s, 0, 0)),
                pl.BlockSpec((1, R, K * BS), lambda s, *_: (s, 0, 0)),
            ],
            out_specs=(
                pl.BlockSpec((owners * BS, WIN), lambda s, *_: (0, 0)),
                pl.BlockSpec((1, BS), lambda s, *_: (0, 0)),
            ),
            scratch_shapes=[pltpu.VMEM((owners * BS, WIN), jnp.float32)],
        ),
        compiler_params=pltpu.CompilerParams(vmem_limit_bytes=56 * 2**20),
    )(links, counts, owner_map, owner_map.reshape(1, NB), kinv, coupling)


def flip(index, bits, size):
    result = 0
    weight = 1
    while weight < size:
        bit = (index // weight) % 2
        if (bits // weight) % 2:
            bit = 1 - bit
        result = result + bit * weight
        weight *= 2
    return result


def exchange_kernel(
    groups, owners, rows_ref, first_ref, codes_ref, all_rows, all_table, all_codes,
    own_send, own_recv, x_send, x_recv, core_send, core_recv,
    table_send, table_recv, meta_send, meta_recv, meta2_send, meta2_recv, local_sem,
):
    g = lax.axis_index("scen")
    o = lax.axis_index("own")
    chips = groups // 2
    core = g % 2
    x = g // 2
    sibling = x * 2 + 1 - core
    xs = [flip(x, b, chips) * 2 + core for b in range(chips)]
    partner = [flip(o, k, owners) for k in range(owners)]

    barrier = pltpu.get_barrier_semaphore()
    for k in range(1, owners):
        pl.semaphore_signal(barrier, inc=1, device_id=(g, partner[k]), device_id_type=MESH)
    others = [flip(g, b, groups) for b in range(1, groups)]
    for other in others:
        pl.semaphore_signal(barrier, inc=1, device_id=(other, o), device_id_type=MESH)
    pl.semaphore_wait(barrier, owners - 1 + groups - 1)

    def remote(src, dst, send, recv, device):
        return pltpu.make_async_remote_copy(
            src_ref=src, dst_ref=dst, send_sem=send, recv_sem=recv,
            device_id=device, device_id_type=MESH,
        )

    own = [None] * owners
    for k in range(1, owners):
        own[k] = remote(
            rows_ref.at[partner[k]], all_rows.at[g, o], own_send.at[k], own_recv.at[k], (g, partner[k])
        )
    meta = [None] * owners
    for k in range(1, owners):
        meta[k] = remote(
            codes_ref, all_codes.at[g, o], meta_send.at[k], meta_recv.at[k], (g, partner[k])
        )
    table = [None] * owners
    for k in range(1, owners):
        table[k] = remote(
            first_ref, all_table.at[o], table_send.at[k], table_recv.at[k], (g, partner[k])
        )
    keep_table = pltpu.make_async_copy(first_ref, all_table.at[o], local_sem.at[2])
    keep_rows = pltpu.make_async_copy(rows_ref.at[o], all_rows.at[g, o], local_sem.at[0])
    keep_meta = pltpu.make_async_copy(codes_ref, all_codes.at[g, o], local_sem.at[1])

    far = list(range(owners // 2, owners))
    near = list(range(1, owners // 2))
    keep_meta.start()
    keep_table.start()
    for k in range(1, owners):
        meta[k].start()
    own[far[0]].start()
    own[far[1]].start()
    keep_rows.start()
    for k in near:
        own[k].start()

    x_copies = {}
    core_copies = {}

    def forward(k):
        h = partner[k]
        src = rows_ref.at[o] if k == 0 else all_rows.at[g, h]
        for b in range(1, chips):
            x_copies[b, k] = remote(
                src, all_rows.at[g, h], x_send.at[b, k], x_recv.at[b, k], (xs[b], o)
            )
            x_copies[b, k].start()
        core_copies[0, k] = remote(
            src, all_rows.at[g, h], core_send.at[0, k], core_recv.at[0, k], (sibling, o)
        )
        core_copies[0, k].start()

    def forward_x(k):
        h = partner[k]
        for b in range(1, chips):
            x_copies[b, k].wait_recv()
            place = all_rows.at[xs[b], h]
            core_copies[b, k] = remote(
                place, place, core_send.at[b, k], core_recv.at[b, k], (sibling, o)
            )
            core_copies[b, k].start()

    forward(0)
    for k in range(1, owners):
        table[k].start()
    meta2 = []
    keep_meta.wait()
    for k in range(1, owners):
        meta[k].wait()
    for b, other in enumerate(others):
        copy = remote(
            all_codes.at[g], all_codes.at[g], meta2_send.at[b], meta2_recv.at[b], (other, o)
        )
        copy.start()
        meta2.append(copy)
    done = [0]
    for k in near:
        own[k].wait_recv()
        forward(k)
        done.append(k)
    behind = 0
    for n, k in enumerate(far):
        if n + 2 < len(far):
            own[k].wait_send()
            own[far[n + 2]].start()
        own[k].wait_recv()
        forward(k)
        done.append(k)
        while behind < len(done) - 2:
            forward_x(done[behind])
            behind += 1
    while behind < len(done):
        forward_x(done[behind])
        behind += 1
    for copy in meta2:
        copy.wait()
    keep_rows.wait()
    keep_table.wait()
    for k in range(1, owners):
        table[k].wait()
    for k in near + far[-2:]:
        own[k].wait_send()
    for k in range(owners):
        for b in range(1, chips):
            x_copies[b, k].wait_send()
        for b in range(chips):
            core_copies[b, k].wait()


def exchange(rows, first_rows, codes, groups, owners):
    any_space = pl.BlockSpec(memory_space=pl.ANY)
    dma = pltpu.SemaphoreType.DMA
    return pl.pallas_call(
        functools.partial(exchange_kernel, groups, owners),
        out_shape=(
            jax.ShapeDtypeStruct((groups, owners, BS, WIN), jnp.bfloat16),
            jax.ShapeDtypeStruct((owners,) + first_rows.shape, jnp.float32),
            jax.ShapeDtypeStruct((groups, owners) + codes.shape, jnp.int32),
        ),
        in_specs=[any_space] * 3,
        out_specs=(any_space,) * 3,
        scratch_shapes=[
            dma((owners,)), dma((owners,)),
            dma((groups // 2, owners)), dma((groups // 2, owners)),
            dma((groups // 2, owners)), dma((groups // 2, owners)),
            dma((owners,)), dma((owners,)),
            dma((owners,)), dma((owners,)),
            dma((groups,)), dma((groups,)),
            dma((3,)),
        ],
        compiler_params=pltpu.CompilerParams(collective_id=0, has_side_effects=True),
    )(rows, first_rows, codes)


def place_kernel(
    blocks, groups, owners, links_ref, counts_ref, codes_ref,
    kinv_ref, coup_ref, residual_ref, table_ref, rows_ref, band_ref, step_ref, held, sems,
):
    s = pl.program_id(0)
    sources = groups * owners
    base = lax.axis_index("scen") * blocks
    me = lax.axis_index("own")

    def code_of(n):
        return codes_ref[n // owners, n % owners, 0, me]

    def copy_of(n):
        return pltpu.make_async_copy(rows_ref.at[n], held.at[n], sems.at[n])

    @pl.when(s == 0)
    def _():
        def begin(n, carry):
            code = code_of(n)
            rank = code // W - base

            @pl.when((code >= 0) & (rank >= 0) & (rank < blocks))
            def _():
                copy_of(n).start()

            return carry

        lax.fori_loop(0, sources, begin, 0)

    count = counts_ref[s]
    parts = []
    for k in range(K):
        row = table_ref[pl.ds(links_ref[s, k], 1), :]
        parts.append(jnp.where(k < count, row, 0.0))
    picked = jnp.broadcast_to(jnp.concatenate(parts, axis=1), (16, K * BS)).astype(jnp.bfloat16)
    product = lax.dot_general(picked, coup_ref[0], NT, preferred_element_type=jnp.float32)
    reduced = (residual_ref[pl.ds(s, 1), :] - product).astype(jnp.bfloat16)
    step = lax.dot_general(reduced, kinv_ref[0], NT, preferred_element_type=jnp.float32)
    step_ref[pl.ds(s, 1), :] = step[:1]

    @pl.when(s < blocks)
    def _():
        band_ref[...] = jnp.zeros_like(band_ref)

        def add(n, carry):
            code = code_of(n)

            @pl.when((code >= 0) & (code // W - base == s))
            def _():
                copy_of(n).wait()
                col = pl.multiple_of((W - 1 - code % W) * BS, BS)
                band_ref[:, pl.ds(col, WIN)] += held[n].astype(jnp.float32)

            return carry

        lax.fori_loop(0, sources, add, 0)


def place(links, counts, codes, kinv, coupling, residual, table, rows, blocks):
    scen_count = kinv.shape[0]
    groups, owners = codes.shape[:2]
    sources = groups * owners
    assert blocks <= scen_count
    return pl.pallas_call(
        functools.partial(place_kernel, blocks, groups, owners),
        out_shape=(
            jax.ShapeDtypeStruct((blocks * BS, BAND), jnp.float32),
            jax.ShapeDtypeStruct((scen_count, R), jnp.float32),
        ),
        grid_spec=pltpu.PrefetchScalarGridSpec(
            num_scalar_prefetch=2,
            grid=(scen_count,),
            in_specs=[
                pl.BlockSpec(memory_space=pltpu.SMEM),
                pl.BlockSpec((1, R, R), lambda s, *_: (s, 0, 0)),
                pl.BlockSpec((1, R, K * BS), lambda s, *_: (s, 0, 0)),
                pl.BlockSpec((scen_count, R), lambda s, *_: (0, 0)),
                pl.BlockSpec((NB, BS), lambda s, *_: (0, 0)),
                pl.BlockSpec(memory_space=pl.ANY),
            ],
            out_specs=(
                pl.BlockSpec((BS, BAND), lambda s, *_: (jnp.minimum(s, blocks - 1), 0)),
                pl.BlockSpec((scen_count, R), lambda s, *_: (0, 0)),
            ),
            scratch_shapes=[
                pltpu.VMEM((sources, BS, WIN), jnp.bfloat16),
                pltpu.SemaphoreType.DMA((sources,)),
            ],
        ),
        compiler_params=pltpu.CompilerParams(vmem_limit_bytes=58 * 2**20),
    )(links, counts, codes, kinv, coupling, residual, table, rows)


def local(kinv, coupling, residual, first_step, links, counts, owner_map):
    groups = lax.axis_size("scen")
    owners = lax.axis_size("own")
    blocks = NB // owners // groups
    rows, codes = windows(links, counts, owner_map, kinv, coupling, owners)
    all_rows, all_table, all_codes = exchange(
        rows.reshape(owners, BS, WIN), first_step.reshape(-1, BS), codes, groups, owners
    )
    band, second_step = place(
        links, counts, all_codes, kinv, coupling, residual, all_table.reshape(NB, BS),
        all_rows.reshape(groups * owners, BS, WIN), blocks,
    )
    return band[None], second_step


def solution(mesh):
    placed = (
        P(("scen", "own"), None, None),
        P(("scen", "own"), None, None),
        P(("scen", "own"), None),
        P("own"),
        P(("scen", "own"), None),
        P(("scen", "own")),
        P(),
    )
    return jax.shard_map(
        local,
        mesh=mesh,
        in_specs=placed,
        out_specs=(P("own", "scen", None), P(("scen", "own"), None)),
        check_vma=False,
    )
```
